256 devices in a mesh: chan: 32 (over y_lo, z, core), stn: 8 (over y_hi, x).
Axes of the slice: x: 4, y: 4 (y_hi: 2, y_lo: 2; y = y_hi * 2 + y_lo), z: 8, core: 2. Of those that a mesh axis runs over, the one named last changes fastest.
Arguments:
- volts: bfloat16 [1024, 2, 98304], P('stn', None, 'chan'), may hold values from -6 to 6
- taps: float32 [16, 256], replicated, may hold values from -1.5 to 1.5
Outputs:
- visibilities: float32 [256, 2, 1024, 1024], P(('chan', 'stn'))
The draws below stay inside these ranges and needn't reach their ends.
All inputs are finite; a program needn't handle non-finite values.
Results may differ from the reference program's by a relative error of at most 0.0035.
Values may be sent and summed in bfloat16 or wider, within the bound.
A program may use at most 128 MiB of HBM per device.

```python
import math
import jax
import jax.numpy as jnp
from jax import lax

INPUTS = 1024
FINE = 256
TAPS = 16
NSPEC = 384


def block_levels(key, dims, shards, smallest, largest):
    factor_of = 1.0
    for dim, parts in shards:
        heights = jax.random.uniform(jax.random.fold_in(jax.random.fold_in(key, 6), dim), (parts,), jnp.float32, smallest / len(shards), largest / len(shards))
        factor_of = factor_of * jnp.repeat(jnp.exp(heights), dims[dim] // parts).reshape((-1,) + (1,) * (len(dims) - 1 - dim))
    return factor_of


def bell_draw(key, extent, deviation, bound, cuts=(), kind=jnp.bfloat16):
    entries = deviation * jax.random.normal(key, extent, jnp.float32)
    if cuts:
        entries = entries * block_levels(key, extent, cuts, -0.22, 0.18)
    return jnp.clip(entries, -bound, bound).astype(kind)


def setup_inputs(seed: int = 0) -> dict:
    keys = jax.random.split(jax.random.key(seed), 3)
    return {
        "volts": bell_draw(keys[0], (INPUTS, 2, NSPEC * FINE), 1.0, 6.0, ((0, 8), (2, 32))),
        "taps": bell_draw(keys[1], (TAPS, FINE), 0.25, 1.5, (), jnp.float32),
    }


def fourier_table(length):
    positions = jnp.arange(length, dtype=jnp.int32)
    phases = positions[:, None] * positions[None, :] % length
    angles = phases.astype(jnp.float32) * (2.0 * math.pi / length)
    cosine = jnp.cos(angles) / math.sqrt(length)
    sine_part = jnp.sin(angles) / math.sqrt(length)
    upper_rows = jnp.concatenate([cosine, sine_part], axis=1)
    lower_rows = jnp.concatenate([-sine_part, cosine], axis=1)
    return jnp.concatenate([upper_rows, lower_rows], axis=0)

def channelize(block_volts, taps, fourier):
    tap_count, length = taps.shape
    row_count = block_volts.shape[0]
    spectra_count = block_volts.shape[2] // length
    shaped = block_volts.reshape(row_count, 2, spectra_count, length)
    padded = jnp.pad(shaped, ((0, 0), (0, 0), (tap_count - 1, 0), (0, 0)))
    filtered = jnp.zeros((row_count, 2, spectra_count, length), jnp.float32)
    for tap_index in range(tap_count):
        begin = tap_count - 1 - tap_index
        filtered = filtered + taps[tap_index] * padded[:, :, begin:begin + spectra_count, :].astype(jnp.float32)
    stacked = filtered.transpose(0, 2, 1, 3).reshape(row_count, spectra_count, 2 * length)
    spectra = jnp.einsum('kl,isl->kis', fourier, stacked, precision=lax.Precision.HIGHEST)
    return spectra.astype(jnp.bfloat16)

def reference(volts, taps):
    inputs = volts.shape[0]
    samples = volts.shape[2]
    length = taps.shape[1]
    spectra_count = samples // length
    fourier = fourier_table(length)
    block_rows = inputs // 4
    blocks = volts.reshape(4, block_rows, 2, samples)
    spectra = lax.map(lambda block_volts: channelize(block_volts, taps, fourier), blocks)
    spectra = spectra.transpose(1, 0, 2, 3).reshape(2 * length, inputs, spectra_count)

    def correlate(pair):
        real_part, imag_part = pair
        right_rows = jnp.concatenate([real_part, imag_part], axis=1)
        lower_rows = jnp.concatenate([imag_part, -real_part], axis=1)
        left_rows = jnp.concatenate([right_rows, lower_rows], axis=0)
        product = jnp.dot(left_rows, right_rows.T, preferred_element_type=jnp.float32)
        return product.reshape(2, inputs, inputs) / spectra_count
    return lax.map(correlate, (spectra[:length], spectra[length:]))
```

```python
import functools
import math

import jax
import jax.numpy as jnp
import numpy as np
from jax import lax
from jax.experimental import pallas as pl
from jax.experimental.pallas import tpu as pltpu
from jax.sharding import PartitionSpec as P

MESH = pl.DeviceIdType.MESH
F32 = jnp.float32
BF16 = jnp.bfloat16

FINE = 256
TAPS = 16
OWN = 12
PRE = 7
POST = 8
LANES = 128
ROWS = 256
GROUP = 8


def fourier_tables():
    index = np.arange(FINE)
    angle = (index[:, None] * index[None, :] % FINE) * (2.0 * math.pi / FINE)
    c, s = np.cos(angle) / math.sqrt(FINE), np.sin(angle) / math.sqrt(FINE)
    whole = np.block([[c, s], [-s, c]]).astype(np.float32)
    high = whole.astype(BF16)
    return high, (whole - high.astype(np.float32)).astype(BF16)


def channelize_kernel(*refs):
    own, fast, slow = refs[:24], refs[24:48], refs[48:64]
    taps, whigh, wlow, stage, window, filtered, xhigh, xlow, turned = refs[64:]
    chan = lax.axis_index("chan")
    core = chan % 2

    def put(at, ref):
        window[at] = ref.reshape(ROWS, LANES)[...]

    def clear(begin, end):
        def step(i, carry):
            window[i] = jnp.zeros((ROWS, LANES), BF16)
            return carry

        lax.fori_loop(begin, end, step, 0)

    @pl.when(core == 0)
    def _():
        for i in range(2 * PRE):
            put(i, slow[2 + i])
        for i in range(24):
            put(2 * PRE + i, own[i])
            put(2 * PRE + 24 + i, fast[i])

    @pl.when(core == 1)
    def _():
        for i in range(6):
            put(i, fast[18 + i])
        for i in range(24):
            put(6 + i, own[i])
        for i in range(2 * POST):
            put(30 + i, slow[i])

    @pl.when(chan == 0)
    def _():
        clear(0, 2 * PRE)

    @pl.when(chan == 31)
    def _():
        clear(0, 30)

    def group(first):
        def filter_rows(i, carry):
            half = i % 2
            rows = pl.ds(pl.multiple_of((i // 2) * 16, 16), 16)
            inputs = [
                window[2 * (first + n) + half, rows, :].astype(F32)
                for n in range(GROUP + TAPS - 1)
            ]
            for j in range(GROUP):
                total = None
                for k in range(TAPS):
                    term = taps[half, pl.ds(k, 1), :] * inputs[j + TAPS - 1 - k]
                    total = term if total is None else total + term
                filtered[half * GROUP + j, rows, :] = total
            return carry

        lax.fori_loop(0, 2 * (ROWS // 16), filter_rows, 0)

        def split(j, carry):
            rows = pl.ds(pl.multiple_of(j * LANES, LANES), LANES)
            for half in range(2):
                for part in range(2):
                    value = filtered[half * GROUP + j, pl.ds(part, LANES, stride=2), :]
                    high = value.astype(BF16)
                    columns = pl.ds((part * 2 + half) * LANES, LANES)
                    xhigh[rows, columns] = high
                    xlow[rows, columns] = (value - high.astype(F32)).astype(BF16)
            return carry

        lax.fori_loop(0, GROUP, split, 0)

        high, low = whigh[...], wlow[...]
        dims = (((1,), (1,)), ((), ()))

        def transform(j, carry):
            inputs = pl.ds(pl.multiple_of(j * 256, 256), 256)
            value = xhigh[inputs, :]
            total = lax.dot_general(high, value, dims, preferred_element_type=F32)
            total += lax.dot_general(low, value, dims, preferred_element_type=F32)
            total += lax.dot_general(high, xlow[inputs, :], dims, preferred_element_type=F32)
            turned[2 * j] = total[:, :LANES]
            turned[2 * j + 1] = total[:, LANES:]
            return carry

        lax.fori_loop(0, GROUP // 2, transform, 0)
        flat = turned.reshape(GROUP * 2 * FINE, LANES)

        def turn(i, carry):
            for n in range(8):
                f = i * 8 + n
                real = flat[pl.ds(f, GROUP, stride=2 * FINE), :]
                imag = flat[pl.ds(FINE + f, GROUP, stride=2 * FINE), :]
                stage[f, 2 * first : 2 * first + 16] = jnp.concatenate([real, imag], axis=0).astype(
                    BF16
                )
            return carry

        lax.fori_loop(0, FINE // 8, turn, 0)

    group(0)

    @pl.when(core == 0)
    def _():
        group(GROUP)

    @pl.when(core == 1)
    def _():
        stage[:, 16:] = jnp.zeros((FINE, 16, LANES), BF16)


def channelize(volts, fast, slow, taps):
    high, low = fourier_tables()
    taps = taps.reshape(TAPS, 2, LANES).transpose(1, 0, 2)
    column = lambda i: pl.BlockSpec((128, 2, LANES), lambda s: (0, 0, i))
    whole = lambda shape: pl.BlockSpec(shape, lambda s: (0,) * len(shape))
    return pl.pallas_call(
        channelize_kernel,
        grid=(1,),
        out_shape=jax.ShapeDtypeStruct((FINE, 32, LANES), BF16),
        in_specs=[column(i) for i in range(24)]
        + [column(i) for i in range(24)]
        + [column(i) for i in range(16)]
        + [whole((2, TAPS, LANES)), whole((512, 512)), whole((512, 512))],
        out_specs=whole((FINE, 32, LANES)),
        scratch_shapes=[
            pltpu.VMEM((62, ROWS, LANES), BF16),
            pltpu.VMEM((2 * GROUP, ROWS, LANES), F32),
            pltpu.VMEM((GROUP * LANES, 2 * FINE), BF16),
            pltpu.VMEM((GROUP * LANES, 2 * FINE), BF16),
            pltpu.VMEM((GROUP, 2 * FINE, LANES), F32),
        ],
        compiler_params=pltpu.CompilerParams(vmem_limit_bytes=48 << 20),
    )(*[volts] * 24, *[fast] * 24, *[slow] * 16, taps, jnp.asarray(high), jnp.asarray(low))


def correlate_kernel(*refs):
    parts, (out, held, turned, crossed) = refs[:8], refs[8:]
    step = pl.program_id(0)
    depth = held.shape[0]

    @pl.when(step == 0)
    def _():
        for g in range(8):
            held[:, g * LANES : (g + 1) * LANES] = parts[g][...].reshape(depth, LANES)
        turned[...] = held[...].T

        def cross(i, carry):
            rows = pl.ds(pl.multiple_of(i * 16, 16), 16)
            block = held[rows, :].astype(F32)
            crossed[rows, :] = jnp.concatenate([-block[8:], block[:8]], axis=0).astype(BF16)
            return carry

        lax.fori_loop(0, depth // 16, cross, 0)

    rows = turned[pl.ds(pl.multiple_of(step * 256, 256), 256), :]
    scale = 1.0 / 384
    out[0, 0] = jnp.dot(rows, held[...], preferred_element_type=F32) * scale
    out[0, 1] = jnp.dot(rows, crossed[...], preferred_element_type=F32) * scale


def correlate(got, shape, part):
    depth = math.prod(shape) // LANES
    return pl.pallas_call(
        correlate_kernel,
        grid=(4,),
        out_shape=jax.ShapeDtypeStruct((1, 2, 1024, 1024), F32),
        in_specs=[pl.BlockSpec(shape, functools.partial(part, g)) for g in range(8)],
        out_specs=pl.BlockSpec((1, 2, 256, 1024), lambda i: (0, 0, i, 0)),
        scratch_shapes=[
            pltpu.VMEM((depth, 1024), BF16),
            pltpu.VMEM((1024, depth), BF16),
            pltpu.VMEM((depth, 1024), BF16),
        ],
        compiler_params=pltpu.CompilerParams(vmem_limit_bytes=48 << 20),
    )(*[got] * 8)


def shards(volts, taps):
    core = lax.axis_index("chan") % 2
    fast = lax.ppermute(volts, "chan", [(i, i ^ 1) for i in range(32)])
    reach = POST * FINE
    edge = jnp.where(core == 0, volts[:, :, :reach], volts[:, :, -reach:])
    slow = lax.ppermute(edge, "chan", [(i, (i + (1 if i % 2 else -1)) % 32) for i in range(32)])
    stage = channelize(volts, fast, slow, taps)
    got = lax.all_to_all(stage, ("chan", "stn"), 0, 0, tiled=True)
    return correlate(
        got.reshape(32, 8, 32, LANES), (32, 1, 32, LANES), lambda g, i: (0, g, 0, 0)
    )


def solution(mesh):
    return jax.shard_map(
        shards,
        mesh=mesh,
        in_specs=(P("stn", None, "chan"), P()),
        out_specs=P(("chan", "stn"), None, None, None),
        check_vma=False,
    )
```

```python
import functools
import math

import jax
import jax.numpy as jnp
import numpy as np
from jax import lax
from jax.experimental import pallas as pl
from jax.experimental.pallas import tpu as pltpu
from jax.sharding import PartitionSpec as P

MESH = pl.DeviceIdType.MESH
F32 = jnp.float32
BF16 = jnp.bfloat16

FINE = 256
TAPS = 16
POST = 8
LANES = 128
ROWS = 256
GROUP = 8
Z_ORDER = (4, 3, 5, 2, 6, 1, 7, 0)


def fourier_tables():
    z, core, y, x = np.unravel_index(np.arange(FINE), (8, 2, 4, 4))
    channel = ((y % 2) * 16 + z * 2 + core) * 8 + (y // 2) * 4 + x
    angle = (channel[:, None] * np.arange(FINE)[None, :] % FINE) * (2.0 * math.pi / FINE)
    c, s = np.cos(angle) / math.sqrt(FINE), np.sin(angle) / math.sqrt(FINE)
    whole = np.block([[c, s], [-s, c]]).astype(np.float32)
    high = whole.astype(BF16)
    return high, (whole - high.astype(np.float32)).astype(BF16)


def filter_group(window, taps, whigh, wlow, stage, filtered, xhigh, xlow, turned):
    def filter_rows(i, carry):
        half = i % 2
        rows = pl.ds(pl.multiple_of((i // 2) * 16, 16), 16)
        inputs = [window[2 * n + half, rows, :].astype(F32) for n in range(GROUP + TAPS - 1)]
        for j in range(GROUP):
            total = None
            for k in range(TAPS):
                term = taps[half, pl.ds(k, 1), :] * inputs[j + TAPS - 1 - k]
                total = term if total is None else total + term
            filtered[half * GROUP + j, rows, :] = total
        return carry

    lax.fori_loop(0, 2 * (ROWS // 16), filter_rows, 0)

    def split(j, carry):
        rows = pl.ds(pl.multiple_of(j * LANES, LANES), LANES)
        for half in range(2):
            for part in range(2):
                value = filtered[half * GROUP + j, pl.ds(part, LANES, stride=2), :]
                high = value.astype(BF16)
                columns = pl.ds((part * 2 + half) * LANES, LANES)
                xhigh[rows, columns] = high
                xlow[rows, columns] = (value - high.astype(F32)).astype(BF16)
        return carry

    lax.fori_loop(0, GROUP, split, 0)

    high, low = whigh[...], wlow[...]
    dims = (((1,), (1,)), ((), ()))

    def transform(j, carry):
        inputs = pl.ds(pl.multiple_of(j * 256, 256), 256)
        value = xhigh[inputs, :]
        total = lax.dot_general(high, value, dims, preferred_element_type=F32)
        total += lax.dot_general(low, value, dims, preferred_element_type=F32)
        total += lax.dot_general(high, xlow[inputs, :], dims, preferred_element_type=F32)
        turned[2 * j] = total[:, :LANES]
        turned[2 * j + 1] = total[:, LANES:]
        return carry

    lax.fori_loop(0, GROUP // 2, transform, 0)
    flat = turned.reshape(GROUP * 2 * FINE, LANES)

    def turn(i, carry):
        for n in range(8):
            f = i * 8 + n
            real = flat[pl.ds(f, GROUP, stride=2 * FINE), :]
            imag = flat[pl.ds(FINE + f, GROUP, stride=2 * FINE), :]
            stage[f] = jnp.concatenate([real, imag], axis=0).astype(BF16)
        return carry

    lax.fori_loop(0, FINE // 8, turn, 0)


def put(window, at, ref):
    window[at] = ref.reshape(ROWS, LANES)[...]


def inner_kernel(*refs):
    own, fast = refs[:22], refs[22:46]
    taps, whigh, wlow, stage, window, *scratch = refs[46:]

    @pl.when(lax.axis_index("chan") % 2 == 0)
    def _():
        for i in range(22):
            put(window, i, own[i])
        for i in range(24):
            put(window, 22 + i, fast[i])
        filter_group(window, taps, whigh, wlow, stage, *scratch)


def edge_kernel(*refs):
    own, fast, slow = refs[:24], refs[24:38], refs[38:54]
    taps, whigh, wlow, stage, window, *scratch = refs[54:]
    chan = lax.axis_index("chan")
    core = chan % 2

    @pl.when(core == 0)
    def _():
        for i in range(14):
            put(window, i, slow[2 + i])
        for i in range(24):
            put(window, 14 + i, own[i])
        for i in range(8):
            put(window, 38 + i, fast[i])

    @pl.when(core == 1)
    def _():
        for i in range(6):
            put(window, i, fast[8 + i])
        for i in range(24):
            put(window, 6 + i, own[i])
        for i in range(16):
            put(window, 30 + i, slow[i])

    def clear(end):
        def step(i, carry):
            window[i] = jnp.zeros((ROWS, LANES), BF16)
            return carry

        lax.fori_loop(0, end, step, 0)

    @pl.when(chan == 0)
    def _():
        clear(14)

    @pl.when(chan == 31)
    def _():
        clear(30)

    filter_group(window, taps, whigh, wlow, stage, *scratch)


def channelize(kernel, columns, tables):
    whole = lambda shape: pl.BlockSpec(shape, lambda s: (0,) * len(shape))
    column = lambda i: pl.BlockSpec((128, 2, LANES), lambda s: (0, 0, i))
    return pl.pallas_call(
        kernel,
        grid=(1,),
        out_shape=jax.ShapeDtypeStruct((FINE, 16, LANES), BF16),
        in_specs=[column(i) for _, i in columns] + [whole(t.shape) for t in tables],
        out_specs=whole((FINE, 16, LANES)),
        scratch_shapes=[
            pltpu.VMEM((46, ROWS, LANES), BF16),
            pltpu.VMEM((2 * GROUP, ROWS, LANES), F32),
            pltpu.VMEM((GROUP * LANES, 2 * FINE), BF16),
            pltpu.VMEM((GROUP * LANES, 2 * FINE), BF16),
            pltpu.VMEM((GROUP, 2 * FINE, LANES), F32),
        ],
        compiler_params=pltpu.CompilerParams(vmem_limit_bytes=40 << 20),
        cost_estimate=pl.CostEstimate(flops=2 << 30, bytes_accessed=16 << 20, transcendentals=0),
    )(*[array for array, _ in columns], *tables)


def spread_kernel(edge, inner, got, middle, send1, recv1, own1, send2, recv2, own2):
    chan, stn = lax.axis_index("chan"), lax.axis_index("stn")
    core, z, ylow = chan % 2, (chan // 2) % 8, chan // 16
    y, x = (stn // 4) * 2 + ylow, stn % 4
    here = y * 4 + x

    def line_device(dz, side):
        return (ylow * 16 + ((z + dz) % 8) * 2 + side, stn)

    def plane_device(i):
        y2, x2 = (y + i // 4) % 4, (x + i) % 4
        return ((y2 % 2) * 16 + z * 2 + core, (y2 // 2) * 4 + x2), y2 * 4 + x2

    barrier = pltpu.get_barrier_semaphore()

    def greet_plane(i, carry):
        pl.semaphore_signal(barrier, inc=1, device_id=plane_device(i)[0], device_id_type=MESH)
        return carry

    for dz in range(8):
        for turn in range(2):
            if dz or turn:
                device = line_device(dz, (core + turn) % 2)
                pl.semaphore_signal(barrier, inc=1, device_id=device, device_id_type=MESH)
    lax.fori_loop(1, 16, greet_plane, 0)
    pl.semaphore_wait(barrier, 30)

    def block(array, dz, side, row, sem):
        start = (((z + dz) % 8) * 2 + side) * 16
        return dict(
            src_ref=array.at[pl.ds(start, 16)],
            dst_ref=middle.at[z, :, pl.ds(row, 16), :],
            send_sem=send1.at[sem],
            recv_sem=recv1.at[sem],
            device_id=line_device(dz, side),
            device_id_type=MESH,
        )

    def blocks(mine, dz):
        out = []
        for side in range(2):
            if dz or side != mine:
                cross = side != mine
                out.append((edge, side, 32 * mine, dz * 6 + mine * 2 + cross))
                if mine == 0:
                    out.append((inner, side, 16, dz * 6 + 4 + cross))
        return out

    def own_blocks(mine):
        pairs = [(edge, 32 * mine)] + ([(inner, 16)] if mine == 0 else [])
        start = (z * 2 + mine) * 16
        return [
            pltpu.make_async_copy(
                array.at[pl.ds(start, 16)], middle.at[z, :, pl.ds(row, 16), :], own1.at[n]
            )
            for n, (array, row) in enumerate(pairs)
        ]

    for mine in range(2):

        @pl.when(core == mine)
        def _(mine=mine):
            for copy in own_blocks(mine):
                copy.start()
            for dz in Z_ORDER:
                for array, side, row, sem in blocks(mine, dz):
                    pltpu.make_async_remote_copy(**block(array, dz, side, row, sem)).start()

    def arrived(mine, dz):
        for source in range(2):
            for array, side, row, sem in blocks(source, dz):
                if side == mine:
                    pltpu.make_async_remote_copy(**block(array, dz, side, row, sem)).wait_recv()

    for dz in Z_ORDER:
        for mine in range(2):

            @pl.when(core == mine)
            def _(mine=mine, dz=dz):
                arrived(mine, dz)
                if dz == 0:
                    for copy in own_blocks(mine):
                        copy.wait()

        source = (z + 8 - dz) % 8

        def forward(i, carry, source=source):
            device, there = plane_device(i)
            pltpu.make_async_remote_copy(
                src_ref=middle.at[source, there],
                dst_ref=got.at[stn, ylow * 8 + source],
                send_sem=send2,
                recv_sem=recv2,
                device_id=device,
                device_id_type=MESH,
            ).start()
            return carry

        lax.fori_loop(1, 16, forward, 0)

    own = pltpu.make_async_copy(middle.at[:, here], got.at[stn, pl.ds(ylow * 8, 8)], own2)
    own.start()
    for mine in range(2):

        @pl.when(core == mine)
        def _(mine=mine):
            for dz in Z_ORDER:
                for array, side, row, sem in blocks(mine, dz):
                    pltpu.make_async_remote_copy(**block(array, dz, side, row, sem)).wait_send()

    own.wait()
    plane = middle.at[:, pl.ds(0, 15)]
    every = pltpu.make_async_remote_copy(
        src_ref=plane,
        dst_ref=plane,
        send_sem=send2,
        recv_sem=recv2,
        device_id=line_device(1, core),
        device_id_type=MESH,
    )
    every.wait_send()
    every.wait_recv()


def spread(edge, inner):
    any_spec = pl.BlockSpec(memory_space=pl.ANY)
    dma = pltpu.SemaphoreType.DMA
    return pl.pallas_call(
        spread_kernel,
        out_shape=jax.ShapeDtypeStruct((8, 16, 48, LANES), BF16),
        in_specs=[any_spec, any_spec],
        out_specs=any_spec,
        scratch_shapes=[
            pltpu.VMEM((8, 16, 48, LANES), BF16),
            dma((48,)),
            dma((48,)),
            dma((2,)),
            dma,
            dma,
            dma,
        ],
        compiler_params=pltpu.CompilerParams(
            collective_id=0, has_side_effects=True, vmem_limit_bytes=16 << 20
        ),
    )(edge, inner)


def correlate_kernel(*refs):
    parts, (out, held, turned, crossed) = refs[:8], refs[8:]
    step = pl.program_id(0)
    depth = held.shape[0]

    @pl.when(step == 0)
    def _():
        for g in range(8):
            held[:, g * LANES : (g + 1) * LANES] = parts[g][...].reshape(depth, LANES)
        turned[...] = held[...].T

        def cross(i, carry):
            rows = pl.ds(pl.multiple_of(i * 16, 16), 16)
            block = held[rows, :].astype(F32)
            crossed[rows, :] = jnp.concatenate([-block[8:], block[:8]], axis=0).astype(BF16)
            return carry

        lax.fori_loop(0, depth // 16, cross, 0)

    rows = turned[pl.ds(pl.multiple_of(step * 256, 256), 256), :]
    scale = 1.0 / 384
    out[0, 0] = jnp.dot(rows, held[...], preferred_element_type=F32) * scale
    out[0, 1] = jnp.dot(rows, crossed[...], preferred_element_type=F32) * scale


def correlate(got, shape, part):
    depth = math.prod(shape) // LANES
    return pl.pallas_call(
        correlate_kernel,
        grid=(4,),
        out_shape=jax.ShapeDtypeStruct((1, 2, 1024, 1024), F32),
        in_specs=[pl.BlockSpec(shape, functools.partial(part, g)) for g in range(8)],
        out_specs=pl.BlockSpec((1, 2, 256, 1024), lambda i: (0, 0, i, 0)),
        scratch_shapes=[
            pltpu.VMEM((depth, 1024), BF16),
            pltpu.VMEM((1024, depth), BF16),
            pltpu.VMEM((depth, 1024), BF16),
        ],
        compiler_params=pltpu.CompilerParams(vmem_limit_bytes=48 << 20),
    )(*[got] * 8)


def shards(volts, taps):
    core = lax.axis_index("chan") % 2
    reach = POST * FINE
    edge = jnp.where(core == 0, volts[:, :, :reach], volts[:, :, -reach:])
    slow = lax.ppermute(edge, "chan", [(i, (i + (1 if i % 2 else -1)) % 32) for i in range(32)])
    fast = lax.ppermute(volts, "chan", [(i, i ^ 1) for i in range(32)])
    high, low = fourier_tables()
    taps = taps.reshape(TAPS, 2, LANES).transpose(1, 0, 2)
    tables = (taps, jnp.asarray(high), jnp.asarray(low))
    inner = channelize(
        inner_kernel,
        [(volts, i) for i in range(2, 24)] + [(fast, i) for i in range(24)],
        tables,
    )
    near = list(range(8)) + list(range(18, 24))
    outer = channelize(
        edge_kernel,
        [(volts, i) for i in range(24)]
        + [(fast, i) for i in near]
        + [(slow, i) for i in range(16)],
        tables,
    )
    got = spread(outer, inner)
    return correlate(got, (1, 16, 48, LANES), lambda g, i: (g, 0, 0, 0))


def solution(mesh):
    return jax.shard_map(
        shards,
        mesh=mesh,
        in_specs=(P("stn", None, "chan"), P()),
        out_specs=P(("chan", "stn"), None, None, None),
        check_vma=False,
    )
```

```python
import functools
import math

import jax
import jax.numpy as jnp
import numpy as np
from jax import lax
from jax.experimental import pallas as pl
from jax.experimental.pallas import tpu as pltpu
from jax.sharding import PartitionSpec as P

MESH = pl.DeviceIdType.MESH
F32 = jnp.float32
BF16 = jnp.bfloat16

FINE = 256
TAPS = 16
POST = 8
LANES = 128
ROWS = 256
GROUP = 8
Z_ORDER = (0, 4, 3, 5, 2, 6, 1, 7)
AHEAD = 3


def fourier_tables():
    z, core, y, x = np.unravel_index(np.arange(FINE), (8, 2, 4, 4))
    channel = ((y % 2) * 16 + z * 2 + core) * 8 + (y // 2) * 4 + x
    angle = (channel[:, None] * np.arange(FINE)[None, :] % FINE) * (2.0 * math.pi / FINE)
    c, s = np.cos(angle) / math.sqrt(FINE), np.sin(angle) / math.sqrt(FINE)
    whole = np.block([[c, s], [-s, c]]).astype(np.float32)
    high = whole.astype(BF16)
    return high, (whole - high.astype(np.float32)).astype(BF16)


def filter_group(window, taps, whigh, wlow, stage, xhigh, xlow, turned):
    def filter_rows(i, carry):
        half, part = i % 2, i // 16
        rows = pl.ds(pl.multiple_of((i // 2) * 16, 16), 16)
        inputs = [window[2 * n + half, rows, :].astype(F32) for n in range(GROUP + TAPS - 1)]
        columns = pl.ds(pl.multiple_of((part * 2 + half) * LANES, LANES), LANES)
        for j in range(GROUP):
            total = None
            for k in range(TAPS):
                term = taps[half, pl.ds(k, 1), :] * inputs[j + TAPS - 1 - k]
                total = term if total is None else total + term
            place = pl.ds(pl.multiple_of(j * LANES + (i // 2) % 8 * 16, 16), 16)
            high = total.astype(BF16)
            xhigh[place, columns] = high
            xlow[place, columns] = (total - high.astype(F32)).astype(BF16)
        return carry

    lax.fori_loop(0, 2 * (ROWS // 16), filter_rows, 0)

    high, low = whigh[...], wlow[...]
    dims = (((1,), (1,)), ((), ()))

    def transform(j, carry):
        inputs = pl.ds(pl.multiple_of(j * 256, 256), 256)
        value = xhigh[inputs, :]
        total = lax.dot_general(high, value, dims, preferred_element_type=F32)
        total += lax.dot_general(low, value, dims, preferred_element_type=F32)
        total += lax.dot_general(high, xlow[inputs, :], dims, preferred_element_type=F32)
        turned[2 * j] = total[:, :LANES]
        turned[2 * j + 1] = total[:, LANES:]
        return carry

    lax.fori_loop(0, GROUP // 2, transform, 0)
    flat = turned.reshape(GROUP * 2 * FINE, LANES)

    def turn(i, carry):
        for n in range(8):
            f = i * 8 + n
            real = flat[pl.ds(f, GROUP, stride=2 * FINE), :]
            imag = flat[pl.ds(FINE + f, GROUP, stride=2 * FINE), :]
            stage[f] = jnp.concatenate([real, imag], axis=0).astype(BF16)
        return carry

    lax.fori_loop(0, FINE // 8, turn, 0)


def put(window, at, ref, begin, count):
    for i in range(count):
        window[at + i] = ref[:, (begin + i) * LANES : (begin + i + 1) * LANES]


def inner_kernel(own, fast, taps, whigh, wlow, stage, window, *scratch):
    @pl.when(lax.axis_index("chan") % 2 == 0)
    def _():
        put(window, 0, own, 2, 22)
        put(window, 22, fast, 0, 24)
        filter_group(window, taps, whigh, wlow, stage, *scratch)


def edge_kernel(own, fast, slow, taps, whigh, wlow, stage, window, *scratch):
    chan = lax.axis_index("chan")
    core = chan % 2

    @pl.when(core == 0)
    def _():
        put(window, 0, slow, 2, 14)
        put(window, 14, own, 0, 24)
        put(window, 38, fast, 0, 8)

    @pl.when(core == 1)
    def _():
        put(window, 0, fast, 18, 6)
        put(window, 6, own, 0, 24)
        put(window, 30, slow, 0, 16)

    def clear(end):
        def step(i, carry):
            window[i] = jnp.zeros((ROWS, LANES), BF16)
            return carry

        lax.fori_loop(0, end, step, 0)

    @pl.when(chan == 0)
    def _():
        clear(14)

    @pl.when(chan == 31)
    def _():
        clear(30)

    filter_group(window, taps, whigh, wlow, stage, *scratch)


def channelize(kernel, *arrays):
    whole = lambda shape: pl.BlockSpec(shape, lambda s: (0,) * len(shape))
    return pl.pallas_call(
        kernel,
        grid=(1,),
        out_shape=jax.ShapeDtypeStruct((FINE, 16, LANES), BF16),
        in_specs=[whole(array.shape) for array in arrays],
        out_specs=whole((FINE, 16, LANES)),
        scratch_shapes=[
            pltpu.VMEM((46, ROWS, LANES), BF16),
            pltpu.VMEM((GROUP * LANES, 2 * FINE), BF16),
            pltpu.VMEM((GROUP * LANES, 2 * FINE), BF16),
            pltpu.VMEM((GROUP, 2 * FINE, LANES), F32),
        ],
        compiler_params=pltpu.CompilerParams(vmem_limit_bytes=40 << 20),
        cost_estimate=pl.CostEstimate(flops=2 << 30, bytes_accessed=16 << 20, transcendentals=0),
    )(*arrays)


def spread_kernel(edge, inner, got, middle, send1, recv1, own1, send2, recv2, own2):
    chan, stn = lax.axis_index("chan"), lax.axis_index("stn")
    core, z, ylow = chan % 2, (chan // 2) % 8, chan // 16
    y, x = (stn // 4) * 2 + ylow, stn % 4
    here = y * 4 + x

    def line_device(dz, side):
        return (ylow * 16 + ((z + dz) % 8) * 2 + side, stn)

    def plane_device(i):
        y2, x2 = (y + i // 4) % 4, (x + i) % 4
        return ((y2 % 2) * 16 + z * 2 + core, (y2 // 2) * 4 + x2), y2 * 4 + x2

    barrier = pltpu.get_barrier_semaphore()

    def greet_plane(i, carry):
        pl.semaphore_signal(barrier, inc=1, device_id=plane_device(i)[0], device_id_type=MESH)
        return carry

    for dz in range(8):
        for turn in range(2):
            if dz or turn:
                device = line_device(dz, (core + turn) % 2)
                pl.semaphore_signal(barrier, inc=1, device_id=device, device_id_type=MESH)
    lax.fori_loop(1, 16, greet_plane, 0)
    pl.semaphore_wait(barrier, 30)

    def block(array, dz, side, row, sem):
        start = (((z + dz) % 8) * 2 + side) * 16
        return dict(
            src_ref=array.at[pl.ds(start, 16)],
            dst_ref=middle.at[z, :, pl.ds(row, 16), :],
            send_sem=send1.at[sem],
            recv_sem=recv1.at[sem],
            device_id=line_device(dz, side),
            device_id_type=MESH,
        )

    def blocks(mine, dz):
        out = []
        for side in range(2):
            if dz or side != mine:
                cross = side != mine
                out.append((edge, side, 32 * mine, dz * 6 + mine * 2 + cross))
                if mine == 0:
                    out.append((inner, side, 16, dz * 6 + 4 + cross))
        return out

    def own_blocks(mine):
        pairs = [(edge, 32 * mine)] + ([(inner, 16)] if mine == 0 else [])
        start = (z * 2 + mine) * 16
        return [
            pltpu.make_async_copy(
                array.at[pl.ds(start, 16)], middle.at[z, :, pl.ds(row, 16), :], own1.at[n]
            )
            for n, (array, row) in enumerate(pairs)
        ]

    def start(n):
        for mine in range(2):

            @pl.when(core == mine)
            def _(mine=mine):
                if n == 0:
                    for copy in own_blocks(mine):
                        copy.start()
                for array, side, row, sem in blocks(mine, Z_ORDER[n]):
                    pltpu.make_async_remote_copy(**block(array, Z_ORDER[n], side, row, sem)).start()

    for n in range(AHEAD):
        start(n)

    def arrived(mine, dz):
        for source in range(2):
            for array, side, row, sem in blocks(source, dz):
                if side == mine:
                    pltpu.make_async_remote_copy(**block(array, dz, side, row, sem)).wait_recv()

    for n, dz in enumerate(Z_ORDER):
        for mine in range(2):

            @pl.when(core == mine)
            def _(mine=mine, dz=dz):
                arrived(mine, dz)
                if dz == 0:
                    for copy in own_blocks(mine):
                        copy.wait()

        source = (z + 8 - dz) % 8

        def forward(i, carry, source=source):
            device, there = plane_device(i)
            pltpu.make_async_remote_copy(
                src_ref=middle.at[source, there],
                dst_ref=got.at[stn, ylow * 8 + source],
                send_sem=send2,
                recv_sem=recv2,
                device_id=device,
                device_id_type=MESH,
            ).start()
            return carry

        lax.fori_loop(1, 16, forward, 0)
        if n + AHEAD < 8:
            start(n + AHEAD)

    own = pltpu.make_async_copy(middle.at[:, here], got.at[stn, pl.ds(ylow * 8, 8)], own2)
    own.start()
    for mine in range(2):

        @pl.when(core == mine)
        def _(mine=mine):
            for dz in Z_ORDER:
                for array, side, row, sem in blocks(mine, dz):
                    pltpu.make_async_remote_copy(**block(array, dz, side, row, sem)).wait_send()

    own.wait()
    plane = middle.at[:, pl.ds(0, 15)]
    every = pltpu.make_async_remote_copy(
        src_ref=plane,
        dst_ref=plane,
        send_sem=send2,
        recv_sem=recv2,
        device_id=line_device(1, core),
        device_id_type=MESH,
    )
    every.wait_send()
    every.wait_recv()


def spread(edge, inner):
    any_spec = pl.BlockSpec(memory_space=pl.ANY)
    dma = pltpu.SemaphoreType.DMA
    return pl.pallas_call(
        spread_kernel,
        out_shape=jax.ShapeDtypeStruct((8, 16, 48, LANES), BF16),
        in_specs=[any_spec, any_spec],
        out_specs=any_spec,
        scratch_shapes=[
            pltpu.VMEM((8, 16, 48, LANES), BF16),
            dma((48,)),
            dma((48,)),
            dma((2,)),
            dma,
            dma,
            dma,
        ],
        compiler_params=pltpu.CompilerParams(
            collective_id=0, has_side_effects=True, vmem_limit_bytes=16 << 20
        ),
    )(edge, inner)


def correlate_kernel(*refs):
    parts, (out, held, turned, crossed) = refs[:8], refs[8:]
    step = pl.program_id(0)
    depth = held.shape[0]

    @pl.when(step == 0)
    def _():
        for g in range(8):
            held[:, g * LANES : (g + 1) * LANES] = parts[g][...].reshape(depth, LANES)
        turned[...] = held[...].T

        def cross(i, carry):
            rows = pl.ds(pl.multiple_of(i * 16, 16), 16)
            block = held[rows, :].astype(F32)
            crossed[rows, :] = jnp.concatenate([-block[8:], block[:8]], axis=0).astype(BF16)
            return carry

        lax.fori_loop(0, depth // 16, cross, 0)

    rows = turned[pl.ds(pl.multiple_of(step * 256, 256), 256), :]
    scale = 1.0 / 384
    out[0, 0] = jnp.dot(rows, held[...], preferred_element_type=F32) * scale
    out[0, 1] = jnp.dot(rows, crossed[...], preferred_element_type=F32) * scale


def correlate(got, shape, part):
    depth = math.prod(shape) // LANES
    return pl.pallas_call(
        correlate_kernel,
        grid=(4,),
        out_shape=jax.ShapeDtypeStruct((1, 2, 1024, 1024), F32),
        in_specs=[pl.BlockSpec(shape, functools.partial(part, g)) for g in range(8)],
        out_specs=pl.BlockSpec((1, 2, 256, 1024), lambda i: (0, 0, i, 0)),
        scratch_shapes=[
            pltpu.VMEM((depth, 1024), BF16),
            pltpu.VMEM((1024, depth), BF16),
            pltpu.VMEM((depth, 1024), BF16),
        ],
        compiler_params=pltpu.CompilerParams(vmem_limit_bytes=48 << 20),
    )(*[got] * 8)


def shards(volts, taps):
    core = lax.axis_index("chan") % 2
    reach = POST * FINE
    by_part = lambda array: array.transpose(1, 0, 2).reshape(ROWS, -1)
    own = by_part(volts)
    edge = jnp.where(core == 0, own[:, :reach], own[:, -reach:])
    slow = lax.ppermute(edge, "chan", [(i, (i + (1 if i % 2 else -1)) % 32) for i in range(32)])
    fast = lax.ppermute(own, "chan", [(i, i ^ 1) for i in range(32)])
    high, low = fourier_tables()
    taps = taps.reshape(TAPS, 2, LANES).transpose(1, 0, 2)
    tables = (taps, jnp.asarray(high), jnp.asarray(low))
    inner = channelize(inner_kernel, own, fast, *tables)
    outer = channelize(edge_kernel, own, fast, slow, *tables)
    got = spread(outer, inner)
    return correlate(got, (1, 16, 48, LANES), lambda g, i: (g, 0, 0, 0))


def solution(mesh):
    return jax.shard_map(
        shards,
        mesh=mesh,
        in_specs=(P("stn", None, "chan"), P()),
        out_specs=P(("chan", "stn"), None, None, None),
        check_vma=False,
    )
```

```python
import functools
import math

import jax
import jax.numpy as jnp
import numpy as np
from jax import lax
from jax.experimental import pallas as pl
from jax.experimental.pallas import tpu as pltpu
from jax.sharding import PartitionSpec as P

MESH = pl.DeviceIdType.MESH
F32 = jnp.float32
BF16 = jnp.bfloat16

FINE = 256
TAPS = 16
POST = 8
LANES = 128
ROWS = 256
GROUP = 8
AHEAD = 2


def fourier_tables():
    y, x, z, core = np.unravel_index(np.arange(FINE), (4, 4, 8, 2))
    channel = ((y % 2) * 16 + z * 2 + core) * 8 + (y // 2) * 4 + x
    angle = (channel[:, None] * np.arange(FINE)[None, :] % FINE) * (2.0 * math.pi / FINE)
    c, s = np.cos(angle) / math.sqrt(FINE), np.sin(angle) / math.sqrt(FINE)
    whole = np.block([[c, s], [-s, c]]).astype(np.float32)
    high = whole.astype(BF16)
    return high, (whole - high.astype(np.float32)).astype(BF16)


def filter_group(window, taps, whigh, wlow, stage, xhigh, xlow, turned):
    def filter_rows(i, carry):
        half, part = i % 2, i // 16
        rows = pl.ds(pl.multiple_of((i // 2) * 16, 16), 16)
        inputs = [window[2 * n + half, rows, :].astype(F32) for n in range(GROUP + TAPS - 1)]
        columns = pl.ds(pl.multiple_of((part * 2 + half) * LANES, LANES), LANES)
        for j in range(GROUP):
            total = None
            for k in range(TAPS):
                term = taps[half, pl.ds(k, 1), :] * inputs[j + TAPS - 1 - k]
                total = term if total is None else total + term
            place = pl.ds(pl.multiple_of(j * LANES + (i // 2) % 8 * 16, 16), 16)
            high = total.astype(BF16)
            xhigh[place, columns] = high
            xlow[place, columns] = (total - high.astype(F32)).astype(BF16)
        return carry

    lax.fori_loop(0, 2 * (ROWS // 16), filter_rows, 0)

    high, low = whigh[...], wlow[...]
    dims = (((1,), (1,)), ((), ()))

    def transform(j, carry):
        inputs = pl.ds(pl.multiple_of(j * 256, 256), 256)
        value = xhigh[inputs, :]
        total = lax.dot_general(high, value, dims, preferred_element_type=F32)
        total += lax.dot_general(low, value, dims, preferred_element_type=F32)
        total += lax.dot_general(high, xlow[inputs, :], dims, preferred_element_type=F32)
        turned[2 * j] = total[:, :LANES]
        turned[2 * j + 1] = total[:, LANES:]
        return carry

    lax.fori_loop(0, GROUP // 2, transform, 0)
    flat = turned.reshape(GROUP * 2 * FINE, LANES)

    def turn(i, carry):
        for n in range(8):
            f = i * 8 + n
            real = flat[pl.ds(f, GROUP, stride=2 * FINE), :]
            imag = flat[pl.ds(FINE + f, GROUP, stride=2 * FINE), :]
            stage[f] = jnp.concatenate([real, imag], axis=0).astype(BF16)
        return carry

    lax.fori_loop(0, FINE // 8, turn, 0)


def put(window, at, ref, begin, count):
    for i in range(count):
        window[at + i] = ref[:, (begin + i) * LANES : (begin + i + 1) * LANES]


def inner_kernel(own, fast, taps, whigh, wlow, stage, window, *scratch):
    @pl.when(lax.axis_index("chan") % 2 == 0)
    def _():
        put(window, 0, own, 2, 22)
        put(window, 22, fast, 0, 24)
        filter_group(window, taps, whigh, wlow, stage, *scratch)


def edge_kernel(own, fast, slow, taps, whigh, wlow, stage, window, *scratch):
    chan = lax.axis_index("chan")
    core = chan % 2

    @pl.when(core == 0)
    def _():
        put(window, 0, slow, 2, 14)
        put(window, 14, own, 0, 24)
        put(window, 38, fast, 0, 8)

    @pl.when(core == 1)
    def _():
        put(window, 0, fast, 18, 6)
        put(window, 6, own, 0, 24)
        put(window, 30, slow, 0, 16)

    def clear(end):
        def step(i, carry):
            window[i] = jnp.zeros((ROWS, LANES), BF16)
            return carry

        lax.fori_loop(0, end, step, 0)

    @pl.when(chan == 0)
    def _():
        clear(14)

    @pl.when(chan == 31)
    def _():
        clear(30)

    filter_group(window, taps, whigh, wlow, stage, *scratch)


def channelize(kernel, *arrays):
    whole = lambda shape: pl.BlockSpec(shape, lambda s: (0,) * len(shape))
    return pl.pallas_call(
        kernel,
        grid=(1,),
        out_shape=jax.ShapeDtypeStruct((FINE, 16, LANES), BF16),
        in_specs=[whole(array.shape) for array in arrays],
        out_specs=whole((FINE, 16, LANES)),
        scratch_shapes=[
            pltpu.VMEM((46, ROWS, LANES), BF16),
            pltpu.VMEM((GROUP * LANES, 2 * FINE), BF16),
            pltpu.VMEM((GROUP * LANES, 2 * FINE), BF16),
            pltpu.VMEM((GROUP, 2 * FINE, LANES), F32),
        ],
        compiler_params=pltpu.CompilerParams(vmem_limit_bytes=40 << 20),
        cost_estimate=pl.CostEstimate(flops=2 << 30, bytes_accessed=16 << 20, transcendentals=0),
    )(*arrays)


def spread_kernel(edge, inner, got, middle, send1, recv1, own1, send2, recv2, own2):
    chan, stn = lax.axis_index("chan"), lax.axis_index("stn")
    core, z, ylow = chan % 2, (chan // 2) % 8, chan // 16
    y, x = (stn // 4) * 2 + ylow, stn % 4
    here = y * 4 + x

    def line_device(dz, side):
        return (ylow * 16 + ((z + dz) % 8) * 2 + side, stn)

    def plane_device(dy, dx):
        y2, x2 = (y + dy) % 4, (x + dx) % 4
        return ((y2 % 2) * 16 + z * 2 + core, (y2 // 2) * 4 + x2), y2 * 4 + x2

    barrier = pltpu.get_barrier_semaphore()
    greet = [line_device(dz, (core + turn) % 2) for dz in range(8) for turn in range(2) if dz or turn]
    greet += [plane_device(i // 4, i % 4)[0] for i in range(1, 16)]
    for device in greet:
        pl.semaphore_signal(barrier, inc=1, device_id=device, device_id_type=MESH)
    pl.semaphore_wait(barrier, 30)

    def plane_copies(mine, dy):
        out = []
        for dx in range(4):
            if dy or dx:
                device, there = plane_device(dy, dx)
                for n, array in enumerate((edge, inner)[: 2 - mine]):
                    sem = (dy * 4 + dx) * 2 + n
                    out.append(
                        pltpu.make_async_remote_copy(
                            src_ref=array.at[pl.ds(there * 16, 16)],
                            dst_ref=middle.at[:, here, pl.ds(16 * n, 16), :],
                            send_sem=send1.at[sem],
                            recv_sem=recv1.at[sem],
                            device_id=device,
                            device_id_type=MESH,
                        )
                    )
        return out

    def own_blocks(mine):
        return [
            pltpu.make_async_copy(
                array.at[pl.ds(here * 16, 16)],
                middle.at[:, here, pl.ds(16 * n, 16), :],
                own1.at[n],
            )
            for n, array in enumerate((edge, inner)[: 2 - mine])
        ]

    def own_group(mine, dy):
        source = (y + 4 - dy) % 4
        return pltpu.make_async_copy(
            middle.at[z * 2 + mine, pl.ds(source * 4, 4), pl.ds(0, 32 - 16 * mine), :],
            got.at[
                pl.ds((source // 2) * 4, 4), (source % 2) * 8 + z, pl.ds(32 * mine, 32 - 16 * mine), :
            ],
            own2.at[dy],
        )

    for mine in range(2):

        @pl.when(core == mine)
        def _(mine=mine):
            rows = 32 - 16 * mine
            for copy in own_blocks(mine):
                copy.start()
            for dy in range(AHEAD):
                for copy in plane_copies(mine, dy):
                    copy.start()
            for dy in range(4):
                for copy in plane_copies(mine, dy):
                    copy.wait_recv()
                if dy == 0:
                    for copy in own_blocks(mine):
                        copy.wait()
                source = (y + 4 - dy) % 4

                def forward(i, carry, source=source):
                    dz, side = (i // 2) * 3 % 8, (core + i) % 2
                    z2 = (z + dz) % 8
                    pltpu.make_async_remote_copy(
                        src_ref=middle.at[
                            z2 * 2 + side, pl.ds(source * 4, 4), pl.ds(0, rows), :
                        ],
                        dst_ref=got.at[
                            pl.ds((source // 2) * 4, 4),
                            (source % 2) * 8 + z,
                            pl.ds(32 * mine, rows),
                            :,
                        ],
                        send_sem=send2,
                        recv_sem=recv2.at[mine],
                        device_id=line_device(dz, side),
                        device_id_type=MESH,
                    ).start()
                    return carry

                lax.fori_loop(1, 16, forward, 0)
                own_group(mine, dy).start()
                if dy + AHEAD < 4:
                    for copy in plane_copies(mine, dy + AHEAD):
                        copy.start()
            for dy in range(4):
                for copy in plane_copies(mine, dy):
                    copy.wait_send()
                own_group(mine, dy).wait()

            def all_of(ref, sem):
                return pltpu.make_async_remote_copy(
                    src_ref=ref,
                    dst_ref=ref,
                    send_sem=send2,
                    recv_sem=recv2.at[sem],
                    device_id=line_device(1, core),
                    device_id_type=MESH,
                )

            all_of(middle.at[pl.ds(0, 15), :, pl.ds(0, rows), :], 0).wait_send()
            all_of(middle.at[pl.ds(0, 7 + mine)], 0).wait_recv()
            all_of(middle.at[pl.ds(0, 8 - mine), :, pl.ds(0, 16), :], 1).wait_recv()


def spread(edge, inner):
    any_spec = pl.BlockSpec(memory_space=pl.ANY)
    dma = pltpu.SemaphoreType.DMA
    return pl.pallas_call(
        spread_kernel,
        out_shape=jax.ShapeDtypeStruct((8, 16, 48, LANES), BF16),
        in_specs=[any_spec, any_spec],
        out_specs=any_spec,
        scratch_shapes=[
            pltpu.VMEM((16, 16, 32, LANES), BF16),
            dma((32,)),
            dma((32,)),
            dma((2,)),
            dma,
            dma((2,)),
            dma((4,)),
        ],
        compiler_params=pltpu.CompilerParams(
            collective_id=0, has_side_effects=True, vmem_limit_bytes=16 << 20
        ),
    )(edge, inner)


def correlate_kernel(*refs):
    parts, (out, held, turned, crossed) = refs[:8], refs[8:]
    step = pl.program_id(0)
    depth = held.shape[0]

    @pl.when(step == 0)
    def _():
        for g in range(8):
            held[:, g * LANES : (g + 1) * LANES] = parts[g][...].reshape(depth, LANES)
        turned[...] = held[...].T

        def cross(i, carry):
            rows = pl.ds(pl.multiple_of(i * 16, 16), 16)
            block = held[rows, :].astype(F32)
            crossed[rows, :] = jnp.concatenate([-block[8:], block[:8]], axis=0).astype(BF16)
            return carry

        lax.fori_loop(0, depth // 16, cross, 0)

    rows = turned[pl.ds(pl.multiple_of(step * 256, 256), 256), :]
    scale = 1.0 / 384
    out[0, 0] = jnp.dot(rows, held[...], preferred_element_type=F32) * scale
    out[0, 1] = jnp.dot(rows, crossed[...], preferred_element_type=F32) * scale


def correlate(got, shape, part):
    depth = math.prod(shape) // LANES
    return pl.pallas_call(
        correlate_kernel,
        grid=(4,),
        out_shape=jax.ShapeDtypeStruct((1, 2, 1024, 1024), F32),
        in_specs=[pl.BlockSpec(shape, functools.partial(part, g)) for g in range(8)],
        out_specs=pl.BlockSpec((1, 2, 256, 1024), lambda i: (0, 0, i, 0)),
        scratch_shapes=[
            pltpu.VMEM((depth, 1024), BF16),
            pltpu.VMEM((1024, depth), BF16),
            pltpu.VMEM((depth, 1024), BF16),
        ],
        compiler_params=pltpu.CompilerParams(vmem_limit_bytes=48 << 20),
    )(*[got] * 8)


def shards(volts, taps):
    core = lax.axis_index("chan") % 2
    reach = POST * FINE
    by_part = lambda array: array.transpose(1, 0, 2).reshape(ROWS, -1)
    own = by_part(volts)
    edge = jnp.where(core == 0, own[:, :reach], own[:, -reach:])
    slow = lax.ppermute(edge, "chan", [(i, (i + (1 if i % 2 else -1)) % 32) for i in range(32)])
    fast = lax.ppermute(own, "chan", [(i, i ^ 1) for i in range(32)])
    high, low = fourier_tables()
    taps = taps.reshape(TAPS, 2, LANES).transpose(1, 0, 2)
    tables = (taps, jnp.asarray(high), jnp.asarray(low))
    inner = channelize(inner_kernel, own, fast, *tables)
    outer = channelize(edge_kernel, own, fast, slow, *tables)
    got = spread(outer, inner)
    return correlate(got, (1, 16, 48, LANES), lambda g, i: (g, 0, 0, 0))


def solution(mesh):
    return jax.shard_map(
        shards,
        mesh=mesh,
        in_specs=(P("stn", None, "chan"), P()),
        out_specs=P(("chan", "stn"), None, None, None),
        check_vma=False,
    )
```
